768 devices in a mesh: gx: 12 (over z), yz: 64 (over x, y, core).
Axes of the slice: x: 4, y: 8, z: 12, core: 2. Of those that a mesh axis runs over, the one named last changes fastest.
Arguments:
- tokens: bfloat16 [768, 18432], P(None, 'gx'), may hold values from -200 to 200
- qkv_weight: bfloat16 [18432, 6656], P('gx', 'yz'), may hold values from -0.046875 to 0.046875
- gate_weight: bfloat16 [18432, 36864], P('gx', 'yz'), may hold values from -0.046875 to 0.046875
- up_weight: bfloat16 [18432, 36864], P('gx', 'yz'), may hold values from -0.046875 to 0.046875
- out_weight: bfloat16 [6144, 18432], P(None, 'yz'), may hold values from -0.3125 to 0.3125
- key_cache: bfloat16 [768, 512, 256], P(('gx', 'yz')), may hold values from -2000 to 2000
- value_cache: bfloat16 [768, 512, 256], P(('gx', 'yz')), may hold values from -24 to 24
- lengths: int32 [768], P(('gx', 'yz')), may hold values from 2 to 512, as said below
Outputs:
- attended: bfloat16 [768, 18432], P('gx', 'yz')
- hidden: bfloat16 [768, 36864], P('gx', 'yz')
- new_kv: bfloat16 [768, 512], P(('gx', 'yz'))
The draws below stay inside these ranges and needn't reach their ends.
Inputs may be any that keep to these rules, and one draw needn't show every extreme that they name: `lengths`: some sequence holds 512 earlier tokens and some other holds 2.
All inputs are finite; a program needn't handle non-finite values.
Results may differ from the reference program's by a relative error of at most 0.012.
The reference program's roundings to bfloat16 on the way (of `qkv`, `q_rot`, `weights` and `context`) count: a program that leaves them out, or rounds other values in their place, can miss the bound.
Values may be sent and summed in bfloat16 or wider, within the bound.
No kernel may reach another device: no remote copies, remote signals or barrier semaphores. Data moves between devices by JAX's collectives and lax.ppermute only.
A program may use at most 64 MiB of HBM per device.

```python
import math
import jax
import jax.numpy as jnp
from jax import lax

D = 18432
HD = 256
H = 24
F = 36864
CACHE = 512
QW = 6144
BATCH = 768


def draw_tokens(key, part):
    key = jax.random.fold_in(key, 11)
    keys = jax.random.split(key, 3)
    base = jnp.clip(jax.random.normal(keys[0], (BATCH, D), jnp.float32), -5.0, 5.0)
    row_scale = jnp.exp(jax.random.uniform(keys[1], (BATCH, 1), jnp.float32, 0.0, math.log(10.0)))
    col_rough = jnp.exp(jax.random.uniform(keys[2], (1, D), jnp.float32, math.log(0.5), math.log(2.0)))
    ramp = jnp.sqrt(1.0 + 2.0 * jnp.arange(D, dtype=jnp.float32)[None, :] / D)
    return (base * row_scale * col_rough * ramp).astype(jnp.bfloat16)


def draw_key_cache(key, part):
    key = jax.random.fold_in(key, 37)
    keys = jax.random.split(key, 1)
    base = jnp.clip(jax.random.normal(keys[0], (BATCH, CACHE, HD), jnp.float32), -6.0, 6.0)
    return base.astype(jnp.bfloat16)


def draw_lengths(key, part):
    key = jax.random.fold_in(key, 23)
    keys = jax.random.split(key, 3)
    drawn = jax.random.randint(keys[0], (BATCH,), 2, CACHE + 1, dtype=jnp.int32)
    first = jax.random.randint(keys[1], (), 0, BATCH, dtype=jnp.int32)
    second = (first + 1 + jax.random.randint(keys[2], (), 0, BATCH - 1, dtype=jnp.int32)) % BATCH
    places = jnp.arange(BATCH, dtype=jnp.int32)
    drawn = jnp.where(places == first, CACHE, drawn)
    drawn = jnp.where(places == second, 2, drawn)
    return drawn.astype(jnp.int32)


def level_of(own_key, dims, shards, least, high):
    loudness = 1.0
    for dim, blocks in shards:
        draws = jax.random.uniform(jax.random.fold_in(jax.random.fold_in(own_key, 6), dim), (blocks,), jnp.float32, least / len(shards), high / len(shards))
        loudness = loudness * jnp.repeat(jnp.exp(draws), dims[dim] // blocks).reshape((-1,) + (1,) * (len(dims) - 1 - dim))
    return loudness


def scatter_about(key, dims, spread, reach, cuts=(), held_as=jnp.bfloat16):
    loudness = level_of(key, dims, cuts, -0.22, 0.18) if cuts else 1.0
    entries = jax.random.normal(key, dims, jnp.float32) * spread * loudness
    return jnp.minimum(jnp.maximum(entries, -reach), reach).astype(held_as)


def setup_inputs(seed: int = 0) -> dict:
    key_of = jax.random.split(jax.random.key(seed), 9)
    tokens = draw_tokens(jax.random.fold_in(key_of[8], 71), 0)
    qkv_weight = scatter_about(key_of[1], (D, QW + 2 * HD), D ** -0.5, 0.046875, ((0, 12), (1, 64)))
    gate_weight = scatter_about(key_of[2], (D, F), D ** -0.5, 0.046875, ((0, 12), (1, 64)))
    up_weight = scatter_about(key_of[3], (D, F), D ** -0.5, 0.046875, ((0, 12), (1, 64)))
    out_weight = scatter_about(key_of[4], (QW, D), (QW // 16) ** -0.5, 0.3125, ((1, 64),))
    key_cache = draw_key_cache(jax.random.fold_in(key_of[8], 71), 0)
    value_cache = scatter_about(key_of[6], (BATCH, CACHE, HD), 4.0, 24.0, ((0, 768),))
    lengths = draw_lengths(jax.random.fold_in(key_of[8], 71), 0)
    return {"tokens": tokens, "qkv_weight": qkv_weight, "gate_weight": gate_weight, "up_weight": up_weight, "out_weight": out_weight, "key_cache": key_cache, "value_cache": value_cache, "lengths": lengths}


EPS = 1e-06

def rotate(values, positions):
    half = values.shape[-1] // 2
    freq = 10000.0 ** (-jnp.arange(half, dtype=jnp.float32) / half)
    angle = positions.astype(jnp.float32)[..., None] * freq
    cosine = jnp.cos(angle)
    sine = jnp.sin(angle)
    first = values[..., :half]
    second = values[..., half:]
    return jnp.concatenate([first * cosine - second * sine, second * cosine + first * sine], axis=-1)

def reference(tokens, qkv_weight, gate_weight, up_weight, out_weight, key_cache, value_cache, lengths):
    tok_wide = tokens.astype(jnp.float32)
    squares = lax.optimization_barrier(jnp.sum(tok_wide * tok_wide, axis=1))
    inv_rms = lax.rsqrt(squares / D + EPS)
    qkv = (jnp.dot(tokens, qkv_weight, preferred_element_type=jnp.float32) * inv_rms[:, None]).astype(jnp.bfloat16)
    queries = qkv[:, :H * HD].reshape(BATCH, H, HD)
    q_rot = rotate(queries.astype(jnp.float32), lengths[:, None]).astype(jnp.bfloat16)
    k_rot = rotate(qkv[:, H * HD:H * HD + HD].astype(jnp.float32), lengths).astype(jnp.bfloat16)
    value_new = qkv[:, H * HD + HD:]
    new_kv = jnp.concatenate([k_rot, value_new], axis=1)
    scale = HD ** (-0.5)
    scores = jnp.einsum('bhd,bjd->bhj', q_rot.astype(jnp.float32), key_cache.astype(jnp.float32)) * scale
    own = jnp.einsum('bhd,bd->bh', q_rot.astype(jnp.float32), k_rot.astype(jnp.float32)) * scale
    valid = jnp.arange(CACHE, dtype=jnp.int32)[None, :] < lengths[:, None]
    masked = jnp.where(valid[:, None, :], scores, -jnp.inf)
    top = jnp.maximum(lax.optimization_barrier(jnp.max(masked, axis=-1)), own)
    expo = jnp.exp(masked - top[..., None])
    expo_own = jnp.exp(own - top)
    total = lax.optimization_barrier(jnp.sum(expo, axis=-1)) + expo_own
    weights = (expo / total[..., None]).astype(jnp.bfloat16)
    weight_own = (expo_own / total).astype(jnp.bfloat16)
    context = jnp.einsum('bhj,bjd->bhd', weights.astype(jnp.float32), value_cache.astype(jnp.float32))
    context = context + weight_own.astype(jnp.float32)[..., None] * value_new.astype(jnp.float32)[:, None, :]
    context = context.astype(jnp.bfloat16).reshape(BATCH, H * HD)
    attended = jnp.dot(context, out_weight, preferred_element_type=jnp.float32).astype(jnp.bfloat16)
    gate = jnp.dot(tokens, gate_weight, preferred_element_type=jnp.float32) * inv_rms[:, None]
    upper = jnp.dot(tokens, up_weight, preferred_element_type=jnp.float32) * inv_rms[:, None]
    hidden = (jax.nn.silu(gate) * upper).astype(jnp.bfloat16)
    return (attended, hidden, new_kv)
```

```python
import jax
import jax.numpy as jnp
from jax import lax
from jax.experimental import pallas as pl
from jax.experimental.pallas import tpu as pltpu
from jax.sharding import Mesh, PartitionSpec as P

D = 18432
EPS = 1e-06
HD = 256
HALF = HD // 2
HEADS = 24
SLOTS = 512
ROWS = 768
GX = 12
X, Y, C = 4, 8, 2
YZ = X * Y * C
SEQS = ROWS // GX
QKV = 104
FFN = 576
MAIN = 512
TAIL = FFN - MAIN
BLOCK = 128
F32 = jnp.float32
BF16 = jnp.bfloat16


def params(mib, **kw):
    return pltpu.CompilerParams(vmem_limit_bytes=mib * 1024 * 1024, **kw)


def vmem(*shape):
    return pl.BlockSpec(shape, lambda *_: (0,) * len(shape))


def project_kernel(tok_ref, qkv_ref, gate_ref, up_ref, ffn_ref, part_ref, mixed):
    @pl.when(pl.program_id(0) == 0)
    def _():
        mixed[...] = jnp.concatenate(
            [
                gate_ref[:, MAIN:],
                up_ref[:, MAIN:],
                qkv_ref[...],
                jnp.zeros((qkv_ref.shape[0], 128 - QKV), BF16),
            ],
            axis=1,
        )

    tok = tok_ref[...]
    wide = tok.astype(F32)
    squares = jnp.sum(wide * wide, axis=1, keepdims=True)
    both = jnp.dot(tok, mixed[...], preferred_element_type=F32)
    ffn_ref[:, :MAIN] = jnp.dot(tok, gate_ref[:, :MAIN], preferred_element_type=F32)
    ffn_ref[:, MAIN : 2 * MAIN] = jnp.dot(tok, up_ref[:, :MAIN], preferred_element_type=F32)
    ffn_ref[:, 2 * MAIN :] = both[:, :128]
    lane = lax.broadcasted_iota(jnp.int32, (BLOCK, 128), 1)
    part_ref[...] = jnp.where(lane == QKV, squares, both[:, 128:])


def project(tokens, qkv_weight, gate_weight, up_weight):
    depth = tokens.shape[1]
    return pl.pallas_call(
        project_kernel,
        grid=(ROWS // BLOCK,),
        in_specs=[
            pl.BlockSpec((BLOCK, depth), lambda i: (i, 0)),
            vmem(depth, QKV),
            vmem(depth, FFN),
            vmem(depth, FFN),
        ],
        out_specs=[
            pl.BlockSpec((BLOCK, 2 * FFN), lambda i: (i, 0)),
            pl.BlockSpec((BLOCK, 128), lambda i: (i, 0)),
        ],
        out_shape=[
            jax.ShapeDtypeStruct((ROWS, 2 * FFN), F32),
            jax.ShapeDtypeStruct((ROWS, 128), F32),
        ],
        scratch_shapes=[pltpu.VMEM((depth, 256), BF16)],
        compiler_params=params(28),
        name="project",
    )(tokens, qkv_weight, gate_weight, up_weight)


def norm_kernel(part_ref, out_ref, inv_ref):
    total = part_ref[0:SEQS, :]
    for k in range(1, GX):
        total = total + part_ref[k * SEQS : (k + 1) * SEQS, :]
    inv = lax.rsqrt(total[:, QKV : QKV + 1] / D + EPS)
    inv_ref[...] = jnp.broadcast_to(inv, (SEQS, 128))
    lane = lax.broadcasted_iota(jnp.int32, (SEQS, 128), 1)
    feats = jnp.where(lane < QKV, total * inv, 0.0).astype(BF16).astype(F32)
    me = (lax.axis_index("x") * Y + lax.axis_index("y")) * C + lax.axis_index("c")
    shift = lax.rem(me * QKV, 128)
    moved = pltpu.roll(feats, shift, 1)
    out_ref[:, :128] = jnp.where(lane >= shift, moved, 0.0).astype(BF16)
    out_ref[:, 128:] = jnp.where(lane < shift, moved, 0.0).astype(BF16)


def norm(part):
    return pl.pallas_call(
        norm_kernel,
        out_shape=[
            jax.ShapeDtypeStruct((SEQS, 256), BF16),
            jax.ShapeDtypeStruct((SEQS, 128), F32),
        ],
        compiler_params=params(8),
        name="norm",
    )(part)


def attend_kernel(len_ref, feat_ref, turn_ref, key_ref, value_ref, ctx_ref, kv_ref):
    length = len_ref[0]
    pad = 32
    feats = jnp.concatenate([feat_ref[:, :128], feat_ref[:, 128:]], axis=0)
    row = lax.broadcasted_iota(jnp.int32, (2 * pad, 2 * YZ), 0)
    col = lax.broadcasted_iota(jnp.int32, (2 * pad, 2 * YZ), 1)
    want = jnp.where(row < pad, 2 * row, 2 * (row - pad) + 1)
    source = jnp.where(col < YZ, col, col - YZ)
    have = ((source * QKV) >> 7) + jnp.where(col < YZ, 0, 1)
    pick = jnp.where(want == have, 1.0, 0.0).astype(BF16)
    halves = jnp.dot(pick, feats, preferred_element_type=F32)
    first = halves[:pad]
    second = halves[pad:]
    cosine = turn_ref[0:1, :]
    sine = turn_ref[1:2, :]
    turned = jnp.concatenate(
        [first * cosine - second * sine, second * cosine + first * sine], axis=1
    ).astype(BF16)
    wide = turned.astype(F32)
    key_new = wide[HEADS : HEADS + 1, :]
    value_new = jnp.concatenate(
        [first[HEADS + 1 : HEADS + 2, :], second[HEADS + 1 : HEADS + 2, :]], axis=1
    )
    scale = HD ** (-0.5)
    own = jnp.sum(wide * key_new, axis=1, keepdims=True) * scale
    scores = (
        lax.dot_general(
            turned, key_ref[0], (((1,), (1,)), ((), ())), preferred_element_type=F32
        )
        * scale
    )
    slot = lax.broadcasted_iota(jnp.int32, (pad, SLOTS), 1)
    masked = jnp.where(slot < length, scores, -jnp.inf)
    top = jnp.maximum(jnp.max(masked, axis=1, keepdims=True), own)
    expo = jnp.exp(masked - top)
    expo_own = jnp.exp(own - top)
    total = jnp.sum(expo, axis=1, keepdims=True) + expo_own
    weights = (expo / total).astype(BF16)
    weight_own = (expo_own / total).astype(BF16).astype(F32)
    context = jnp.dot(weights, value_ref[0], preferred_element_type=F32) + weight_own * value_new
    context = jnp.concatenate([context[:HEADS, :HALF], context[:HEADS, HALF:]], axis=0).astype(BF16)
    for k in range(X * Y):
        ctx_ref[k] = context
    kv_ref[...] = jnp.concatenate([key_new, value_new], axis=1).astype(BF16)


def attend(feats, turn, key_cache, value_cache, lengths):
    return pl.pallas_call(
        attend_kernel,
        in_specs=[pl.BlockSpec(memory_space=pltpu.SMEM)]
        + [pl.BlockSpec(memory_space=pltpu.VMEM)] * 4,
        out_specs=[pl.BlockSpec(memory_space=pltpu.VMEM)] * 2,
        out_shape=[
            jax.ShapeDtypeStruct((X * Y, 2 * HEADS, HALF), BF16),
            jax.ShapeDtypeStruct((1, 2 * HD), BF16),
        ],
        compiler_params=params(8),
        name="attend",
    )(lengths, feats, turn, key_cache, value_cache)


def output_kernel(ctx_ref, weight_ref, out_ref):
    flat = ctx_ref[...].reshape(YZ, 2 * HEADS * HALF)
    ordered = jnp.concatenate(
        [
            flat[:, (half * HEADS + head) * HALF : (half * HEADS + head + 1) * HALF]
            for head in range(HEADS)
            for half in range(2)
        ],
        axis=1,
    )
    out = jnp.dot(ordered, weight_ref[...], preferred_element_type=F32).astype(BF16)
    row = lax.broadcasted_iota(jnp.int32, (YZ, YZ), 0)
    col = lax.broadcasted_iota(jnp.int32, (YZ, YZ), 1)
    pick = jnp.where(col == (row % C) * (X * Y) + row // C, 1.0, 0.0).astype(BF16)
    out_ref[...] = jnp.dot(pick, out, preferred_element_type=F32).astype(BF16)


def output(context, out_weight):
    return pl.pallas_call(
        output_kernel,
        out_shape=jax.ShapeDtypeStruct((YZ, out_weight.shape[1]), BF16),
        compiler_params=params(20),
        name="output",
    )(context, out_weight)


def hidden_kernel(ffn_ref, inv_ref, out_ref):
    inv = inv_ref[:, 0:1]
    gate = ffn_ref[:, :MAIN] * inv
    up = ffn_ref[:, MAIN : 2 * MAIN] * inv
    out_ref[:, :MAIN] = (gate * lax.logistic(gate) * up).astype(BF16)
    last = ffn_ref[:, 2 * MAIN :] * inv
    tail = last * lax.logistic(last) * pltpu.roll(last, TAIL, 1)
    out_ref[:, MAIN:] = tail[:, :TAIL].astype(BF16)


def hidden_of(ffn, inv):
    return pl.pallas_call(
        hidden_kernel,
        out_shape=jax.ShapeDtypeStruct((SEQS, FFN), BF16),
        compiler_params=params(8),
        name="hidden",
    )(ffn, inv)


def on_device(
    tokens, qkv_weight, gate_weight, up_weight, out_weight, key_cache, value_cache, lengths
):
    freq = 10000.0 ** (-jnp.arange(HALF, dtype=F32) / HALF)
    angle = lengths.astype(F32)[:, None] * freq
    turn = jnp.concatenate([jnp.cos(angle), jnp.sin(angle)], axis=0)
    ffn, part = project(tokens, qkv_weight, gate_weight, up_weight)
    ffn = lax.psum_scatter(ffn, "gx", scatter_dimension=0, tiled=True)
    part = lax.all_to_all(part, "gx", 0, 0, tiled=True)
    feats, inv = norm(part)
    feats = lax.all_to_all(feats, ("x", "y", "c"), 0, 0, tiled=True)
    context, new_kv = attend(feats, turn, key_cache, value_cache, lengths)
    context = lax.all_to_all(context, ("x", "y"), 0, 0, tiled=True)
    context = lax.all_gather(context, "c", axis=0, tiled=True)
    attended = output(context, out_weight)
    hidden = hidden_of(ffn, inv)
    return (attended, hidden, new_kv)


def solution(mesh):
    fine = Mesh(mesh.devices.reshape(GX, X, Y, C), ("gx", "x", "y", "c"))
    yz = ("x", "y", "c")
    every = ("gx", "x", "y", "c")
    return jax.shard_map(
        on_device,
        mesh=fine,
        in_specs=(
            P(None, "gx"),
            P("gx", yz),
            P("gx", yz),
            P("gx", yz),
            P(None, yz),
            P(every, None, None),
            P(every, None, None),
            P(every),
        ),
        out_specs=(P("gx", yz), P("gx", yz), P(every, None)),
        check_vma=False,
    )
```

```python
import jax
import jax.numpy as jnp
from jax import lax
from jax.experimental import pallas as pl
from jax.experimental.pallas import tpu as pltpu
from jax.sharding import Mesh, PartitionSpec as P

D = 18432
EPS = 1e-06
HD = 256
HALF = HD // 2
HEADS = 24
SLOTS = 512
ROWS = 768
GX = 12
X, Y, C = 4, 8, 2
YZ = X * Y * C
SEQS = ROWS // GX
QKV = 104
FFN = 576
MAIN = 512
TAIL = FFN - MAIN
BLOCK = 128
F32 = jnp.float32
BF16 = jnp.bfloat16


def params(mib, **kw):
    return pltpu.CompilerParams(vmem_limit_bytes=mib * 1024 * 1024, **kw)


def vmem(*shape):
    return pl.BlockSpec(shape, lambda *_: (0,) * len(shape))


def dot_rows(left, right):
    return lax.dot_general(left, right, (((1,), (1,)), ((), ())), preferred_element_type=F32)


def project_kernel(tok_ref, qkv_ref, gate_ref, up_ref, ffn_ref, part_ref, mixed):
    @pl.when(pl.program_id(0) == 0)
    def _():
        mixed[:TAIL] = gate_ref[MAIN:]
        mixed[TAIL : 2 * TAIL] = up_ref[MAIN:]
        fill = jnp.zeros((128 - QKV, qkv_ref.shape[1]), F32)
        mixed[2 * TAIL :] = jnp.concatenate([qkv_ref[...].astype(F32), fill], axis=0).astype(BF16)

    tok = tok_ref[...]
    wide = tok.astype(F32)
    squares = jnp.sum(wide * wide, axis=1, keepdims=True)
    both = dot_rows(tok, mixed[...])
    ffn_ref[:, :MAIN] = dot_rows(tok, gate_ref[:MAIN])
    ffn_ref[:, MAIN : 2 * MAIN] = dot_rows(tok, up_ref[:MAIN])
    ffn_ref[:, 2 * MAIN :] = both[:, :128]
    lane = lax.broadcasted_iota(jnp.int32, (BLOCK, 128), 1)
    part_ref[...] = jnp.where(lane == QKV, squares, both[:, 128:])


def project(tokens, qkv_rows, gate_rows, up_rows):
    depth = tokens.shape[1]
    return pl.pallas_call(
        project_kernel,
        grid=(ROWS // BLOCK,),
        in_specs=[
            pl.BlockSpec((BLOCK, depth), lambda i: (i, 0)),
            vmem(QKV, depth),
            vmem(FFN, depth),
            vmem(FFN, depth),
        ],
        out_specs=[
            pl.BlockSpec((BLOCK, 2 * FFN), lambda i: (i, 0)),
            pl.BlockSpec((BLOCK, 128), lambda i: (i, 0)),
        ],
        out_shape=[
            jax.ShapeDtypeStruct((ROWS, 2 * FFN), F32),
            jax.ShapeDtypeStruct((ROWS, 128), F32),
        ],
        scratch_shapes=[pltpu.VMEM((256, depth), BF16)],
        compiler_params=params(56),
        name="project",
    )(tokens, qkv_rows, gate_rows, up_rows)


def norm_kernel(part_ref, out_ref, inv_ref):
    total = part_ref[0:SEQS, :]
    for k in range(1, GX):
        total = total + part_ref[k * SEQS : (k + 1) * SEQS, :]
    inv = lax.rsqrt(total[:, QKV : QKV + 1] / D + EPS)
    inv_ref[...] = jnp.broadcast_to(inv, (SEQS, 128))
    lane = lax.broadcasted_iota(jnp.int32, (SEQS, 128), 1)
    feats = jnp.where(lane < QKV, total * inv, 0.0).astype(BF16).astype(F32)
    me = (lax.axis_index("x") * Y + lax.axis_index("y")) * C + lax.axis_index("c")
    out_ref[...] = pltpu.roll(feats, lax.rem(me * QKV, 128), 1)


def norm(part):
    return pl.pallas_call(
        norm_kernel,
        out_shape=[
            jax.ShapeDtypeStruct((SEQS, 128), F32),
            jax.ShapeDtypeStruct((SEQS, 128), F32),
        ],
        compiler_params=params(8),
        name="norm",
    )(part)


def attend_kernel(len_ref, feat_ref, turn_ref, key_ref, value_ref, ctx_ref, kv_ref):
    length = len_ref[0]
    pad = 32
    rolled = feat_ref[...]
    start = (lax.broadcasted_iota(jnp.int32, (YZ, 128), 0) * QKV) & 127
    wrapped = lax.broadcasted_iota(jnp.int32, (YZ, 128), 1) < start
    feats = jnp.concatenate(
        [jnp.where(wrapped, 0.0, rolled), jnp.where(wrapped, rolled, 0.0)], axis=0
    ).astype(BF16)
    row = lax.broadcasted_iota(jnp.int32, (2 * pad, 2 * YZ), 0)
    col = lax.broadcasted_iota(jnp.int32, (2 * pad, 2 * YZ), 1)
    want = jnp.where(row < pad, 2 * row, 2 * (row - pad) + 1)
    source = jnp.where(col < YZ, col, col - YZ)
    have = ((source * QKV) >> 7) + jnp.where(col < YZ, 0, 1)
    pick = jnp.where(want == have, 1.0, 0.0).astype(BF16)
    halves = jnp.dot(pick, feats, preferred_element_type=F32)
    first = halves[:pad]
    second = halves[pad:]
    cosine = turn_ref[0:1, :]
    sine = turn_ref[1:2, :]
    turned = jnp.concatenate(
        [first * cosine - second * sine, second * cosine + first * sine], axis=1
    ).astype(BF16)
    wide = turned.astype(F32)
    key_new = wide[HEADS : HEADS + 1, :]
    value_new = jnp.concatenate(
        [first[HEADS + 1 : HEADS + 2, :], second[HEADS + 1 : HEADS + 2, :]], axis=1
    )
    scale = HD ** (-0.5)
    own = jnp.sum(wide * key_new, axis=1, keepdims=True) * scale
    scores = (
        lax.dot_general(
            turned, key_ref[0], (((1,), (1,)), ((), ())), preferred_element_type=F32
        )
        * scale
    )
    slot = lax.broadcasted_iota(jnp.int32, (pad, SLOTS), 1)
    masked = jnp.where(slot < length, scores, -jnp.inf)
    top = jnp.maximum(jnp.max(masked, axis=1, keepdims=True), own)
    expo = jnp.exp(masked - top)
    expo_own = jnp.exp(own - top)
    total = jnp.sum(expo, axis=1, keepdims=True) + expo_own
    weights = (expo / total).astype(BF16)
    weight_own = (expo_own / total).astype(BF16).astype(F32)
    context = jnp.dot(weights, value_ref[0], preferred_element_type=F32) + weight_own * value_new
    context = jnp.concatenate([context[:HEADS, :HALF], context[:HEADS, HALF:]], axis=0).astype(BF16)
    row = lax.broadcasted_iota(jnp.int32, (2 * HEADS, 2 * HEADS), 0)
    col = lax.broadcasted_iota(jnp.int32, (2 * HEADS, 2 * HEADS), 1)
    weave = jnp.where(col == (row % 2) * HEADS + row // 2, 1.0, 0.0).astype(BF16)
    context = jnp.dot(weave, context, preferred_element_type=F32).astype(BF16)
    for k in range(X * Y):
        ctx_ref[k] = context
    kv_ref[...] = jnp.concatenate([key_new, value_new], axis=1).astype(BF16)


def attend(feats, turn, key_cache, value_cache, lengths):
    return pl.pallas_call(
        attend_kernel,
        in_specs=[pl.BlockSpec(memory_space=pltpu.SMEM)]
        + [pl.BlockSpec(memory_space=pltpu.VMEM)] * 4,
        out_specs=[pl.BlockSpec(memory_space=pltpu.VMEM)] * 2,
        out_shape=[
            jax.ShapeDtypeStruct((X * Y, 2 * HEADS, HALF), BF16),
            jax.ShapeDtypeStruct((1, 2 * HD), BF16),
        ],
        compiler_params=params(8),
        name="attend",
    )(lengths, feats, turn, key_cache, value_cache)


def output_kernel(ctx_ref, weight_ref, out_ref):
    flat = ctx_ref[...].reshape(YZ, 2 * HEADS * HALF)
    out = dot_rows(flat, weight_ref[...]).astype(BF16)
    row = lax.broadcasted_iota(jnp.int32, (YZ, YZ), 0)
    col = lax.broadcasted_iota(jnp.int32, (YZ, YZ), 1)
    pick = jnp.where(col == (row % C) * (X * Y) + row // C, 1.0, 0.0).astype(BF16)
    out_ref[...] = jnp.dot(pick, out, preferred_element_type=F32).astype(BF16)


def output(context, out_rows):
    return pl.pallas_call(
        output_kernel,
        out_shape=jax.ShapeDtypeStruct((YZ, out_rows.shape[0]), BF16),
        compiler_params=params(20),
        name="output",
    )(context, out_rows)


def hidden_kernel(ffn_ref, inv_ref, out_ref):
    inv = inv_ref[:, 0:1]
    gate = ffn_ref[:, :MAIN] * inv
    up = ffn_ref[:, MAIN : 2 * MAIN] * inv
    out_ref[:, :MAIN] = (gate * lax.logistic(gate) * up).astype(BF16)
    last = ffn_ref[:, 2 * MAIN :] * inv
    tail = last * lax.logistic(last) * pltpu.roll(last, TAIL, 1)
    out_ref[:, MAIN:] = tail[:, :TAIL].astype(BF16)


def hidden_of(ffn, inv):
    return pl.pallas_call(
        hidden_kernel,
        out_shape=jax.ShapeDtypeStruct((SEQS, FFN), BF16),
        compiler_params=params(56),
        name="hidden",
    )(ffn, inv)


def on_device(
    tokens, qkv_weight, gate_weight, up_weight, out_weight, key_cache, value_cache, lengths
):
    freq = 10000.0 ** (-jnp.arange(HALF, dtype=F32) / HALF)
    angle = lengths.astype(F32)[:, None] * freq
    turn = jnp.concatenate([jnp.cos(angle), jnp.sin(angle)], axis=0)
    ffn, part = project(tokens, qkv_weight.T, gate_weight.T, up_weight.T)
    ffn = lax.psum_scatter(ffn, "gx", scatter_dimension=0, tiled=True)
    part = lax.all_to_all(part, "gx", 0, 0, tiled=True)
    feats, inv = norm(part)
    feats = lax.all_to_all(feats, ("x", "y", "c"), 0, 0, tiled=True)
    context, new_kv = attend(feats, turn, key_cache, value_cache, lengths)
    context = lax.all_to_all(context, ("x", "y"), 0, 0, tiled=True)
    context = lax.all_gather(context, "c", axis=0, tiled=True)
    attended = output(context, out_weight.T)
    hidden = hidden_of(ffn, inv)
    return (attended, hidden, new_kv)


def solution(mesh):
    fine = Mesh(mesh.devices.reshape(GX, X, Y, C), ("gx", "x", "y", "c"))
    yz = ("x", "y", "c")
    every = ("gx", "x", "y", "c")
    return jax.shard_map(
        on_device,
        mesh=fine,
        in_specs=(
            P(None, "gx"),
            P("gx", yz),
            P("gx", yz),
            P("gx", yz),
            P(None, yz),
            P(every, None, None),
            P(every, None, None),
            P(every),
        ),
        out_specs=(P("gx", yz), P("gx", yz), P(every, None)),
        check_vma=False,
    )
```

```python
import jax
import jax.numpy as jnp
from jax import lax
from jax.experimental import pallas as pl
from jax.experimental.pallas import tpu as pltpu
from jax.sharding import Mesh, PartitionSpec as P

D = 18432
EPS = 1e-06
HD = 256
HALF = HD // 2
HEADS = 24
SLOTS = 512
ROWS = 768
GX = 12
X, Y, C = 4, 8, 2
YZ = X * Y * C
SEQS = ROWS // GX
QKV = 104
FFN = 576
MAIN = 512
TAIL = FFN - MAIN
WIDE = 256
BLOCK = 384
SMALL = 128
F32 = jnp.float32
BF16 = jnp.bfloat16
WIRE = BF16


def params(mib, **kw):
    return pltpu.CompilerParams(vmem_limit_bytes=mib * 1024 * 1024, **kw)


def dot_rows(left, right):
    return lax.dot_general(left, right, (((1,), (1,)), ((), ())), preferred_element_type=F32)


def fetch(source, target, sem):
    copy = pltpu.make_async_copy(source, target, sem)
    copy.start()
    return copy


def qkv_kernel(tok_hbm, qkv_hbm, part_hbm, tok, qkv, part, sem_in, sem_out):
    weight = fetch(qkv_hbm, qkv, sem_in.at[0])
    blocks = [pl.ds(i * SMALL, SMALL) for i in range(ROWS // SMALL)]
    loads = [fetch(tok_hbm.at[r], tok.at[r], sem_in.at[1 + i]) for i, r in enumerate(blocks)]
    weight.wait()
    fill = jnp.zeros((128 - QKV, qkv.shape[1]), F32)
    padded = jnp.concatenate([qkv[...].astype(F32), fill], axis=0).astype(BF16)
    lane = lax.broadcasted_iota(jnp.int32, (SMALL, 128), 1)
    stores = []
    for i, r in enumerate(blocks):
        loads[i].wait()
        wide = tok[r, :].astype(F32)
        squares = jnp.sum(wide * wide, axis=1, keepdims=True)
        part[r, :] = jnp.where(lane == QKV, squares, dot_rows(tok[r, :], padded))
        stores.append(fetch(part.at[r], part_hbm.at[r], sem_out.at[i]))
    for copy in stores:
        copy.wait()


def project_qkv(tokens, qkv_rows):
    depth = tokens.shape[1]
    steps = ROWS // SMALL
    return pl.pallas_call(
        qkv_kernel,
        in_specs=[pl.BlockSpec(memory_space=pltpu.HBM)] * 2,
        out_specs=pl.BlockSpec(memory_space=pltpu.HBM),
        out_shape=jax.ShapeDtypeStruct((ROWS, 128), F32),
        scratch_shapes=[
            pltpu.VMEM((ROWS, depth), BF16),
            pltpu.VMEM((QKV, depth), BF16),
            pltpu.VMEM((ROWS, 128), F32),
            pltpu.SemaphoreType.DMA((1 + steps,)),
            pltpu.SemaphoreType.DMA((steps,)),
        ],
        compiler_params=params(62),
        name="project_qkv",
    )(tokens, qkv_rows)


def ffn_kernel(tok_hbm, gate_hbm, up_hbm, ffn_hbm, tok, rows, ffn, sem_in, sem_out):
    loads = []
    for n in range(4):
        weight = (gate_hbm, up_hbm)[n // 2]
        loads.append(fetch(weight.at[pl.ds(n % 2 * WIDE, WIDE)], rows.at[n], sem_in.at[n]))
        if n == 0:
            blocks = [pl.ds(i * BLOCK, BLOCK) for i in range(ROWS // BLOCK)]
            tokens = [
                fetch(tok_hbm.at[r], tok.at[r], sem_in.at[6 + i]) for i, r in enumerate(blocks)
            ]
    last = [
        fetch(gate_hbm.at[pl.ds(MAIN, TAIL)], rows.at[4, pl.ds(0, TAIL)], sem_in.at[4]),
        fetch(up_hbm.at[pl.ds(MAIN, TAIL)], rows.at[4, pl.ds(TAIL, TAIL)], sem_in.at[5]),
    ]
    stores = []

    def put(r, columns):
        place = (r, pl.ds(*columns))
        stores.append(fetch(ffn.at[place], ffn_hbm.at[place], sem_out.at[len(stores)]))

    for n in range(4):
        loads[n].wait()
        for i, r in enumerate(blocks):
            if n == 0:
                tokens[i].wait()
            ffn[r, pl.ds(n * WIDE, WIDE)] = dot_rows(tok[r, :], rows[n]).astype(ffn.dtype)
            if n % 2 == 1:
                put(r, ((n - 1) * WIDE, 2 * WIDE))
    for copy in last:
        copy.wait()
    for r in blocks:
        ffn[r, pl.ds(2 * MAIN, 128)] = dot_rows(tok[r, :], rows[4, :128]).astype(ffn.dtype)
        put(r, (2 * MAIN, 128))
    for copy in stores:
        copy.wait()


def project_ffn(tokens, gate_rows, up_rows):
    depth = tokens.shape[1]
    steps = ROWS // BLOCK
    return pl.pallas_call(
        ffn_kernel,
        in_specs=[pl.BlockSpec(memory_space=pltpu.HBM)] * 3,
        out_specs=pl.BlockSpec(memory_space=pltpu.HBM),
        out_shape=jax.ShapeDtypeStruct((ROWS, 2 * FFN), WIRE),
        scratch_shapes=[
            pltpu.VMEM((ROWS, depth), BF16),
            pltpu.VMEM((5, WIDE, depth), BF16),
            pltpu.VMEM((ROWS, 2 * FFN), WIRE),
            pltpu.SemaphoreType.DMA((6 + steps,)),
            pltpu.SemaphoreType.DMA((3 * steps,)),
        ],
        compiler_params=params(62),
        cost_estimate=pl.CostEstimate(
            flops=4 * ROWS * depth * FFN, bytes_accessed=10_000_000, transcendentals=0
        ),
        name="project_ffn",
    )(tokens, gate_rows, up_rows)


def my_shift():
    me = (lax.axis_index("x") * Y + lax.axis_index("y")) * C + lax.axis_index("c")
    return lax.rem(me * QKV, 128)


def norm_kernel(part_ref, out_ref):
    total = part_ref[0:SEQS, :]
    for k in range(1, GX):
        total = total + part_ref[k * SEQS : (k + 1) * SEQS, :]
    inv = lax.rsqrt(total[:, QKV : QKV + 1] / D + EPS)
    lane = lax.broadcasted_iota(jnp.int32, (SEQS, 128), 1)
    feats = jnp.where(lane == QKV, inv, (total * inv).astype(BF16).astype(F32))
    out_ref[...] = pltpu.roll(feats, my_shift(), 1)


def norm(part):
    return pl.pallas_call(
        norm_kernel,
        out_shape=jax.ShapeDtypeStruct((SEQS, 128), F32),
        compiler_params=params(62),
        name="norm",
    )(part)


def attend_kernel(
    len_ref, feat_hbm, turn_hbm, key_hbm, value_hbm, ctx_hbm, kv_ref, feat, turn, key, value, ctx, sem_in, sem_out
):
    near = [fetch(feat_hbm, feat, sem_in.at[0]), fetch(turn_hbm, turn, sem_in.at[1])]
    keys = fetch(key_hbm.at[0], key, sem_in.at[2])
    values = fetch(value_hbm.at[0], value, sem_in.at[3])
    for copy in near:
        copy.wait()
    length = len_ref[0]
    pad = 32
    rolled = feat[...]
    start = (lax.broadcasted_iota(jnp.int32, (YZ, 128), 0) * QKV) & 127
    lane = lax.broadcasted_iota(jnp.int32, (YZ, 128), 1)
    here = (lane >= start) & (lane < start + QKV)
    beyond = lane < start + QKV - 128
    feats = jnp.concatenate(
        [jnp.where(here, rolled, 0.0), jnp.where(beyond, rolled, 0.0)], axis=0
    ).astype(BF16)
    row = lax.broadcasted_iota(jnp.int32, (2 * pad, 2 * YZ), 0)
    col = lax.broadcasted_iota(jnp.int32, (2 * pad, 2 * YZ), 1)
    want = jnp.where(row < pad, 2 * row, 2 * (row - pad) + 1)
    source = jnp.where(col < YZ, col, col - YZ)
    have = ((source * QKV) >> 7) + jnp.where(col < YZ, 0, 1)
    pick = jnp.where(want == have, 1.0, 0.0).astype(BF16)
    halves = jnp.dot(pick, feats, preferred_element_type=F32)
    first = halves[:pad]
    second = halves[pad:]
    cosine = turn[0:1, :]
    sine = turn[1:2, :]
    turned = jnp.concatenate(
        [first * cosine - second * sine, second * cosine + first * sine], axis=1
    ).astype(BF16)
    wide = turned.astype(F32)
    key_new = wide[HEADS : HEADS + 1, :]
    value_new = jnp.concatenate(
        [first[HEADS + 1 : HEADS + 2, :], second[HEADS + 1 : HEADS + 2, :]], axis=1
    )
    kv_ref[...] = jnp.concatenate([key_new, value_new], axis=1).astype(BF16)
    scale = HD ** (-0.5)
    own = jnp.sum(wide * key_new, axis=1, keepdims=True) * scale
    slot = lax.broadcasted_iota(jnp.int32, (pad, SLOTS), 1)
    keys.wait()
    scores = dot_rows(turned, key[...]) * scale
    masked = jnp.where(slot < length, scores, -jnp.inf)
    top = jnp.maximum(jnp.max(masked, axis=1, keepdims=True), own)
    expo = jnp.exp(masked - top)
    expo_own = jnp.exp(own - top)
    total = jnp.sum(expo, axis=1, keepdims=True) + expo_own
    weights = (expo / total).astype(BF16)
    weight_own = (expo_own / total).astype(BF16).astype(F32)
    values.wait()
    context = jnp.dot(weights, value[...], preferred_element_type=F32) + weight_own * value_new
    context = jnp.concatenate([context[:HEADS, :HALF], context[:HEADS, HALF:]], axis=0).astype(BF16)
    row = lax.broadcasted_iota(jnp.int32, (2 * HEADS, 2 * HEADS), 0)
    col = lax.broadcasted_iota(jnp.int32, (2 * HEADS, 2 * HEADS), 1)
    weave = jnp.where(col == (row % 2) * HEADS + row // 2, 1.0, 0.0).astype(BF16)
    ctx[...] = jnp.dot(weave, context, preferred_element_type=F32).astype(BF16)
    stores = [fetch(ctx, ctx_hbm.at[k], sem_out.at[k]) for k in range(X * Y)]
    for copy in stores:
        copy.wait()


def attend(feats, turn, key_cache, value_cache, lengths):
    return pl.pallas_call(
        attend_kernel,
        in_specs=[pl.BlockSpec(memory_space=pltpu.SMEM)]
        + [pl.BlockSpec(memory_space=pltpu.HBM)] * 4,
        out_specs=[
            pl.BlockSpec(memory_space=pltpu.HBM),
            pl.BlockSpec(memory_space=pltpu.VMEM),
        ],
        out_shape=[
            jax.ShapeDtypeStruct((X * Y, 2 * HEADS, HALF), BF16),
            jax.ShapeDtypeStruct((1, 2 * HD), BF16),
        ],
        scratch_shapes=[
            pltpu.VMEM((YZ, 128), F32),
            pltpu.VMEM((2, HALF), F32),
            pltpu.VMEM((SLOTS, HD), BF16),
            pltpu.VMEM((SLOTS, HD), BF16),
            pltpu.VMEM((2 * HEADS, HALF), BF16),
            pltpu.SemaphoreType.DMA((4,)),
            pltpu.SemaphoreType.DMA((X * Y,)),
        ],
        compiler_params=params(62),
        name="attend",
    )(lengths, feats, turn, key_cache, value_cache)


def output_kernel(ctx_ref, rows_ref, out_ref):
    flat = ctx_ref[...].reshape(YZ, 2 * HEADS * HALF)
    out = dot_rows(flat, rows_ref[...]).astype(BF16)
    row = lax.broadcasted_iota(jnp.int32, (YZ, YZ), 0)
    col = lax.broadcasted_iota(jnp.int32, (YZ, YZ), 1)
    pick = jnp.where(col == (row % C) * (X * Y) + row // C, 1.0, 0.0).astype(BF16)
    out_ref[...] = jnp.dot(pick, out, preferred_element_type=F32).astype(BF16)


def output(context, out_rows):
    return pl.pallas_call(
        output_kernel,
        out_shape=jax.ShapeDtypeStruct((YZ, out_rows.shape[0]), BF16),
        compiler_params=params(20),
        name="output",
    )(context, out_rows)


def hidden_kernel(ffn_ref, feat_ref, out_ref):
    lane = lax.broadcasted_iota(jnp.int32, (SEQS, 128), 1)
    spare = lax.rem(my_shift() + QKV, 128)
    inv = jnp.sum(jnp.where(lane == spare, feat_ref[...], 0.0), axis=1, keepdims=True)
    gate = ffn_ref[:, :MAIN].astype(F32) * inv
    up = ffn_ref[:, MAIN : 2 * MAIN].astype(F32) * inv
    out_ref[:, :MAIN] = (gate * lax.logistic(gate) * up).astype(BF16)
    last = ffn_ref[:, 2 * MAIN :].astype(F32) * inv
    tail = last * lax.logistic(last) * pltpu.roll(last, TAIL, 1)
    out_ref[:, MAIN:] = tail[:, :TAIL].astype(BF16)


def hidden_of(ffn, feats):
    return pl.pallas_call(
        hidden_kernel,
        out_shape=jax.ShapeDtypeStruct((SEQS, FFN), BF16),
        compiler_params=params(62),
        name="hidden",
    )(ffn, feats)


def on_device(
    tokens, qkv_weight, gate_weight, up_weight, out_weight, key_cache, value_cache, lengths
):
    freq = 10000.0 ** (-jnp.arange(HALF, dtype=F32) / HALF)
    angle = lengths.astype(F32)[:, None] * freq
    turn = jnp.concatenate([jnp.cos(angle), jnp.sin(angle)], axis=0)
    part = project_qkv(tokens, qkv_weight.T)
    part = lax.all_to_all(part, "gx", 0, 0, tiled=True)
    ffn = project_ffn(tokens, gate_weight.T, up_weight.T)
    ffn = lax.psum_scatter(ffn, "gx", scatter_dimension=0, tiled=True)
    mine = norm(part)
    feats = lax.all_to_all(mine, ("x", "y", "c"), 0, 0, tiled=True)
    context, new_kv = attend(feats, turn, key_cache, value_cache, lengths)
    context = lax.all_to_all(context, ("x", "y"), 0, 0, tiled=True)
    context = lax.all_gather(context, "c", axis=0, tiled=True)
    attended = output(context, out_weight.T)
    hidden = hidden_of(ffn, mine)
    return (attended, hidden, new_kv)


def solution(mesh):
    fine = Mesh(mesh.devices.reshape(GX, X, Y, C), ("gx", "x", "y", "c"))
    yz = ("x", "y", "c")
    every = ("gx", "x", "y", "c")
    return jax.shard_map(
        on_device,
        mesh=fine,
        in_specs=(
            P(None, "gx"),
            P("gx", yz),
            P("gx", yz),
            P("gx", yz),
            P(None, yz),
            P(every, None, None),
            P(every, None, None),
            P(every),
        ),
        out_specs=(P("gx", yz), P("gx", yz), P(every, None)),
        check_vma=False,
    )
```
